32 devices in a mesh: groups: 2 (over y), tiles: 16 (over z, x, core).
Axes of the slice: x: 2, y: 2, z: 4, core: 2. Of those that a mesh axis runs over, the one named last changes fastest.
Arguments:
- ocean_state: float32 [3, 4, 256, 4352], P(None, 'groups', 'tiles'), parts along dimension 1, may hold values from -6 to 6
- ice_dynamics: float32 [32, 10, 128, 128], P('tiles', 'groups'), parts along dimension 1, may hold values from -3 to 3
- ice_thickness: float32 [32, 10, 128, 128], P('tiles', 'groups'), parts along dimension 1, may hold values from 0.2 to 1
- ice_table: int32 [32, 2], P('groups'), parts along dimension 0, may hold values from -1 to 67, as said below
- land_mask: int32 [136], P('groups'), parts along dimension 0, may hold values from 0 to 1, as said below
Outputs:
- ocean_next: float32 [3, 4, 256, 4352], P(None, 'groups', 'tiles'), parts along dimension 1
- ice_next: float32 [32, 10, 128, 128], P('tiles', 'groups'), parts along dimension 1
The draws below stay inside these ranges and needn't reach their ends.
There are 2 independent parts, one for each index of `groups`. The reference program is written for one: setup_inputs(seed, part) draws one part's arguments, and reference() takes and returns one part's arrays. A program takes and returns all parts, laid end to end along the dimension named above; each array names one. Nothing has to cross between parts.
Inputs may be any that keep to these rules, and one draw needn't show every extreme that they name: `ice_table`: entries are block ids or -1; filled entries are distinct blocks that are not land; an owner's filled slots come first and lie in different rows of blocks; at least a quarter of the owners fill all 2 slots and one owner holds none. `land_mask`: every row of blocks has at least as many blocks that are not land as ice_table places in it.
All inputs are finite; a program needn't handle non-finite values.
Results may differ from the reference program's by a relative error of at most 0.000078.
Values sent between devices are 32-bit elements; how exact they have to be, the bound alone decides.
A program may use at most 64 MiB of HBM per device.

```python
import math
import jax
import jax.numpy as jnp
from jax import lax

BLK = 128
NBX = 34
LEV = 2
NCAT = 5
NSUB = 8
NY = 256
NBY = 2
SLOTS = 2
NX = 4352
ICE_SLOTS = 32
N_TILES = 16


def row_order(row_key):
    return jax.random.permutation(row_key, NBX).astype(jnp.int32)


def layout(key):
    order_key, load_key, rows_key, land_key = jax.random.split(key, 4)
    owner_rank = jax.random.permutation(order_key, N_TILES).astype(jnp.int32)
    light_load = jax.random.randint(load_key, (N_TILES,), 1, min(3, SLOTS) + 1).astype(jnp.int32)
    owner_loads = jnp.where(owner_rank < N_TILES // 4, SLOTS, jnp.where(owner_rank == N_TILES - 1, 0, light_load)).astype(jnp.int32)
    first_filled = (jnp.cumsum(owner_loads) - owner_loads).astype(jnp.int32)
    filled_total = jnp.sum(owner_loads).astype(jnp.int32)
    row_most = ((filled_total + NBY - 1) // NBY).astype(jnp.int32)
    land_top = jnp.broadcast_to(NBX - row_most + 1, (NBY,)).astype(jnp.int32)
    land_count = jax.random.randint(land_key, (NBY,), 0, land_top).astype(jnp.int32)
    orders = jax.vmap(row_order)(jax.random.split(rows_key, NBY))
    column_rank = jnp.argsort(orders, axis=1).astype(jnp.int32)
    land_cells = (column_rank < land_count[:, None]).astype(jnp.int32).reshape(-1)
    slot_index = jnp.arange(SLOTS, dtype=jnp.int32)
    filled_index = first_filled[:, None] + slot_index[None, :]
    block_row = (filled_index % NBY).astype(jnp.int32)
    row_place = (filled_index // NBY).astype(jnp.int32)
    position = jnp.minimum(land_count[block_row] + row_place, NBX - 1).astype(jnp.int32)
    block_column = orders[block_row, position]
    ice_slots = jnp.where(slot_index[None, :] < owner_loads[:, None], block_row * NBX + block_column, -1)
    return (ice_slots.astype(jnp.int32), land_cells)


def draw_ice_table(key, part):
    ice_slots, land_cells = layout(key)
    return ice_slots


def draw_land_mask(key, part):
    ice_slots, land_cells = layout(key)
    return land_cells


def block_levels(own_key, extent, cuts, least, top_value):
    loudness, own = 1.0, jax.random.fold_in(own_key, 6)
    for dim, parts in cuts:
        draws = jnp.exp(jax.random.uniform(jax.random.fold_in(own, dim), (parts,), jnp.float32, least / len(cuts), top_value / len(cuts)))
        loudness = loudness * jnp.repeat(draws, extent[dim] // parts).reshape([-1 if axis == dim else 1 for axis in range(len(extent))])
    return loudness


def bell_draw(key, shape, width, reach, cuts=(), held_as=jnp.bfloat16):
    loudness = block_levels(key, shape, cuts, -0.22, 0.18) if cuts else 1.0
    result = jax.random.normal(key, shape, jnp.float32) * width * loudness
    return jnp.minimum(jnp.maximum(result, -reach), reach).astype(held_as)


def setup_inputs(seed: int = 0, part: int = 0) -> dict:
    key_list = jax.random.split(jax.random.key(seed), 6)
    own_keys = jax.random.split(jax.random.fold_in(key_list[5], part), 6)
    ocean_state = bell_draw(own_keys[0], (3, LEV, NY, NX), 1.0, 6.0, ((2, 16),), jnp.float32)
    ice_dynamics = bell_draw(own_keys[1], (ICE_SLOTS, 5, BLK, BLK), 0.5, 3.0, ((0, 16),), jnp.float32)
    ice_thickness = jnp.clip(jnp.exp(math.log(1.0) - 1.609438 * jax.random.uniform(own_keys[2], (ICE_SLOTS, NCAT, BLK, BLK), jnp.float32) ** block_levels(own_keys[2], (ICE_SLOTS, NCAT, BLK, BLK), ((0, 16),), -0.2, 0.2)), 0.2, 1.0)
    ice_table = draw_ice_table(jax.random.fold_in(jax.random.fold_in(key_list[5], part), 71), part)
    land_mask = draw_land_mask(jax.random.fold_in(jax.random.fold_in(key_list[5], part), 71), part)
    return {"ocean_state": ocean_state, "ice_dynamics": ice_dynamics, "ice_thickness": ice_thickness, "ice_table": ice_table, "land_mask": land_mask}


TIME_STEP = 0.1
MIX_HORIZ = 0.5
MIX_VERT = 0.25
CORIOLIS = 0.5
STRESS_GAIN = 2.0
RELAXATION = 0.2
ICE_STEP = 0.5
DRAG_COEFF = 1.0
ECC_SQUARED = 4.0
DELTA_FLOOR = 0.25
STRENGTH_SCALE = 0.25
HEAT_RATE = 0.5
FREEZING = -1.0
CATEGORY_WEIGHTS = (0.5, 0.75, 1.0, 1.25, 1.5)

def slope_east(values):
    widths = [(0, 0)] * (values.ndim - 1) + [(1, 1)]
    padded = jnp.pad(values, widths)
    return 0.5 * (padded[..., 2:] - padded[..., :-2])

def slope_north(values):
    widths = [(0, 0)] * (values.ndim - 2) + [(1, 1), (0, 0)]
    padded = jnp.pad(values, widths)
    return 0.5 * (padded[..., 2:, :] - padded[..., :-2, :])

def ice_block(currents, thickness, dynamics):
    ocean_u = currents[0]
    ocean_v = currents[1]
    weights = jnp.asarray(CATEGORY_WEIGHTS, dtype=thickness.dtype).reshape(-1, 1, 1)
    total_thick = lax.optimization_barrier(jnp.sum(thickness, axis=0))
    strength = STRENGTH_SCALE * lax.optimization_barrier(jnp.sum(weights * thickness, axis=0))
    ice_cover = 1.0 - jnp.exp(-total_thick)
    inertia = total_thick / ICE_STEP
    ice_u = dynamics[0]
    ice_v = dynamics[1]
    stress_sum = dynamics[2]
    stress_diff = dynamics[3]
    stress_shear = dynamics[4]
    for substep in range(NSUB):
        east_u = slope_east(ice_u)
        north_v = slope_north(ice_v)
        north_u = slope_north(ice_u)
        east_v = slope_east(ice_v)
        divergence = east_u + north_v
        tension = east_u - north_v
        shearing = north_u + east_v
        delta_norm = jnp.sqrt(divergence * divergence + (tension * tension + shearing * shearing) / ECC_SQUARED + DELTA_FLOOR)
        bulk_viscosity = strength / (2.0 * delta_norm)
        shear_viscosity = bulk_viscosity / ECC_SQUARED
        stress_sum = (1.0 - RELAXATION) * stress_sum + RELAXATION * (bulk_viscosity * divergence - 0.5 * strength)
        stress_diff = (1.0 - RELAXATION) * stress_diff + RELAXATION * (shear_viscosity * tension)
        stress_shear = (1.0 - RELAXATION) * stress_shear + RELAXATION * (shear_viscosity * shearing)
        force_x = 0.5 * (slope_east(stress_sum) + slope_east(stress_diff)) + slope_north(stress_shear)
        force_y = 0.5 * (slope_north(stress_sum) - slope_north(stress_diff)) + slope_east(stress_shear)
        relative_u = ocean_u - ice_u
        relative_v = ocean_v - ice_v
        water_drag = DRAG_COEFF * jnp.sqrt(relative_u * relative_u + relative_v * relative_v + 0.0001)
        denominator = inertia + water_drag
        next_u = (inertia * ice_u + force_x + water_drag * ocean_u + CORIOLIS * total_thick * ice_v) / denominator
        next_v = (inertia * ice_v + force_y + water_drag * ocean_v - CORIOLIS * total_thick * ice_u) / denominator
        ice_u = next_u
        ice_v = next_v
    relative_u = ocean_u - ice_u
    relative_v = ocean_v - ice_v
    water_drag = DRAG_COEFF * jnp.sqrt(relative_u * relative_u + relative_v * relative_v + 0.0001)
    stress_x = water_drag * (ice_u - ocean_u)
    stress_y = water_drag * (ice_v - ocean_v)
    dynamics_next = jnp.stack([ice_u, ice_v, stress_sum, stress_diff, stress_shear])
    return (dynamics_next, stress_x, stress_y, ice_cover)

def tendency(padded):
    centre = padded[:, :, 1:-1, :]
    upper_rows = padded[:, :, 2:, :]
    lower_rows = padded[:, :, :-2, :]
    east_cells = jnp.roll(centre, -1, axis=3)
    west_cells = jnp.roll(centre, 1, axis=3)
    laplace = upper_rows + lower_rows + east_cells + west_cells - 4.0 * centre
    grad_x = 0.5 * (east_cells - west_cells)
    grad_y = 0.5 * (upper_rows - lower_rows)
    advection = centre[1] * grad_x + centre[2] * grad_y
    zero_level = jnp.zeros_like(centre[:, :1])
    upward_diff = jnp.concatenate([centre[:, 1:] - centre[:, :-1], zero_level], axis=1)
    downward_diff = jnp.concatenate([zero_level, centre[:, :-1] - centre[:, 1:]], axis=1)
    rotation = CORIOLIS * jnp.stack([jnp.zeros_like(centre[0]), centre[2], -centre[1]])
    return MIX_HORIZ * laplace - advection + MIX_VERT * (upward_diff + downward_diff) + rotation

def reference(ocean_state, ice_dynamics, ice_thickness, ice_table, land_mask):
    padded = jnp.pad(ocean_state, ((0, 0), (0, 0), (1, 1), (0, 0)))
    tendencies = tendency(padded)
    surface = ocean_state[:, 0]
    block_ids = ice_table.reshape(-1).astype(jnp.int32)
    present = block_ids >= 0
    safe_ids = jnp.where(present, block_ids, 0).astype(jnp.int32)
    row_start = (safe_ids // NBX * BLK).astype(jnp.int32)
    col_start = (safe_ids % NBX * BLK).astype(jnp.int32)
    anchor = jnp.zeros((), jnp.int32)

    def one_block(inputs):
        top_row, left_col, thickness, dynamics = inputs
        local_fields = lax.dynamic_slice(surface, (anchor, top_row, left_col), (3, BLK, BLK))
        dynamics_next, stress_x, stress_y, ice_cover = ice_block(local_fields[1:], thickness, dynamics)
        heat_flux = HEAT_RATE * ice_cover * (FREEZING - local_fields[0])
        return (dynamics_next, jnp.stack([heat_flux, stress_x, stress_y]))
    ice_out, returned = lax.map(one_block, (row_start, col_start, ice_thickness, ice_dynamics))
    ice_next = jnp.where(present[:, None, None, None], ice_out, 0.0)

    def place_block(block_index, forcing):
        region = lax.dynamic_slice(forcing, (anchor, row_start[block_index], col_start[block_index]), (3, BLK, BLK))
        update = jnp.where(present[block_index], returned[block_index], region)
        return lax.dynamic_update_slice(forcing, update, (anchor, row_start[block_index], col_start[block_index]))
    forcing = lax.fori_loop(0, block_ids.shape[0], place_block, jnp.zeros_like(surface))
    forcing_gain = jnp.asarray((1.0, STRESS_GAIN, STRESS_GAIN), dtype=surface.dtype).reshape(3, 1, 1)
    forcing = forcing * forcing_gain
    tendencies = tendencies.at[:, 0].add(forcing)
    wet_blocks = 1.0 - land_mask.reshape(NBY, NBX).astype(ocean_state.dtype)
    wet_cells = jnp.broadcast_to(wet_blocks[:, None, :, None], (NBY, BLK, NBX, BLK)).reshape(NBY * BLK, NBX * BLK)
    keep_mask = jnp.stack([jnp.ones_like(wet_cells), wet_cells, wet_cells])[:, None]
    ocean_next = (ocean_state + TIME_STEP * wet_cells * tendencies) * keep_mask
    return (ocean_next, ice_next)
```

```python
import functools

import jax
import jax.numpy as jnp
from jax import lax
from jax.experimental import pallas as pl
from jax.experimental.pallas import tpu as pltpu
from jax.sharding import PartitionSpec as P

BLK = 128
NSUB = 8
TIME_STEP = 0.1
MIX_HORIZ = 0.5
MIX_VERT = 0.25
CORIOLIS = 0.5
STRESS_GAIN = 2.0
RELAXATION = 0.2
ICE_STEP = 0.5
STRENGTH_SCALE = 0.25
HEAT_RATE = 0.5
FREEZING = -1.0
CATEGORY_WEIGHTS = (0.5, 0.75, 1.0, 1.25, 1.5)
PAD = 8
STRIP = 32
MESH = pl.DeviceIdType.MESH


def loop(count, body):
    def step(i, carry):
        body(i)
        return carry

    lax.fori_loop(0, count, step, 0)


def kernel(
    n, columns, levels, slots, rows,
    table, land, ocean_h, dyn_h, thick_h, ocean_o, ice_o,
    oc, acc, dy, th, hs, hr, pk, ar, cpk, car, bpk, bar, st, cf, io, owner_of,
    load_sem, store_sem, ocean_sem, early_sem, late_sem, fs, fr, cs, cr, bs, br, hss, hrs,
):
    me = lax.axis_index("tiles")
    sources = BLK // rows
    block_rows = n // sources
    my_row = me // sources
    my_part = lax.rem(me, sources)
    base = my_row * columns

    def lanes(c):
        return pl.ds(pl.multiple_of(c * BLK, BLK), BLK)

    def load_ocean(c):
        return pltpu.make_async_copy(ocean_h.at[:, :, :, lanes(c)], oc.at[c], ocean_sem.at[c])

    load_thick = pltpu.make_async_copy(thick_h, th, load_sem.at[0])
    load_dyn = pltpu.make_async_copy(dyn_h, dy, load_sem.at[1])
    loop(columns, lambda c: load_ocean(c).start())
    load_thick.start()
    load_dyn.start()

    barrier = pltpu.get_barrier_semaphore()

    def greet(k):
        peer = lax.rem(me + 1 + k, n)
        pl.semaphore_signal(barrier, inc=1, device_id={"tiles": peer}, device_id_type=MESH)

    loop(n - 1, greet)

    def remote(src, dst, ssem, rsem, slot_there, peer):
        return pltpu.make_async_remote_copy(
            src_ref=src.at[peer], dst_ref=dst.at[slot_there], send_sem=ssem.at[peer],
            recv_sem=rsem.at[slot_there], device_id={"tiles": peer}, device_id_type=MESH,
        )

    def send(src, dst, ssem, rsem, peer):
        @pl.when(peer != me)
        def _():
            remote(src, dst, ssem, rsem, me, peer).start()

    def wait_recv(src, dst, ssem, rsem, peer):
        @pl.when(peer != me)
        def _():
            remote(src, dst, ssem, rsem, peer, peer).wait_recv()

    def wait_send(src, dst, ssem, rsem, peer):
        @pl.when(peer != me)
        def _():
            remote(src, dst, ssem, rsem, me, peer).wait_send()

    def member(row, i):
        return row * sources + lax.rem(my_part + i, sources)

    def row_of(j):
        return lax.rem(my_row + j, block_rows)

    loop(columns, lambda c: load_ocean(c).wait())

    def pack(o):
        col = 0
        for s in range(slots):
            rel = table[o, s] - base
            col = jnp.where((rel >= 0) & (rel < columns), rel, col)
        pk[o, 0] = oc[col, 1, 0]
        pk[o, 1] = oc[col, 2, 0]

    loop(n, pack)
    ar[me] = pk[me]
    blank = jnp.zeros((1, BLK), jnp.float32)

    def edges(c):
        tops = [oc[c, f, k, rows - 1 : rows] for f in range(3) for k in range(levels)]
        ends = [oc[c, f, k, 0:1] for f in range(3) for k in range(levels)]
        more = [blank] * (hs.shape[2] - len(tops))
        hs[0, c] = jnp.concatenate(tops + more, axis=0)
        hs[1, c] = jnp.concatenate(ends + more, axis=0)

    loop(columns, edges)

    pl.semaphore_wait(barrier, n - 1)

    def send_fwd(q):
        send(pk, ar, fs, fr, member(row_of(1 + q // sources), lax.rem(q, sources)))

    loop(n, send_fwd)

    def halo(i, peer):
        return pltpu.make_async_remote_copy(
            src_ref=hs.at[i], dst_ref=hr.at[i], send_sem=hss.at[i], recv_sem=hrs.at[i],
            device_id={"tiles": peer}, device_id_type=MESH,
        )

    up = jnp.minimum(me + 1, n - 1)
    down = jnp.maximum(me - 1, 0)

    @pl.when(me < n - 1)
    def _():
        halo(0, up).start()

    @pl.when(me > 0)
    def _():
        halo(1, down).start()

    @pl.when(me == 0)
    def _():
        hr[0] = jnp.zeros(hr.shape[1:], jnp.float32)

    @pl.when(me == n - 1)
    def _():
        hr[1] = jnp.zeros(hr.shape[1:], jnp.float32)

    def find(row):
        slot = jnp.int32(0)
        valid = jnp.int32(0)
        for s in range(slots):
            rel = table[me, s] - row * columns
            hit = (rel >= 0) & (rel < columns)
            slot = jnp.where(hit, s, slot)
            valid = jnp.where(hit, 1, valid)
        return slot, valid

    load_thick.wait()
    load_dyn.wait()

    def prepare(j):
        row = row_of(j)
        slot, valid = find(row)
        keep = valid.astype(jnp.float32)
        for r in range(0, BLK, STRIP):
            cut = pl.ds(r, STRIP)
            parts = [th[slot, k, cut, :] for k in range(len(CATEGORY_WEIGHTS))]
            total = parts[0]
            weighted = CATEGORY_WEIGHTS[0] * parts[0]
            for weight, part in zip(CATEGORY_WEIGHTS[1:], parts[1:]):
                total = total + part
                weighted = weighted + weight * part
            cf[j, 0, cut, :] = total
            cf[j, 1, cut, :] = (0.5 * RELAXATION * STRENGTH_SCALE) * weighted
            cover = keep * (1.0 - jnp.exp(-total))
            for i in range(STRIP // rows):
                cpk[row * sources + r // rows + i] = cover[i * rows : (i + 1) * rows]
            for f in range(5):
                st[j, f, pl.ds(PAD + r, STRIP), :] = dy[slot, f, cut, :]
        for f in range(5):
            st[j, f, 0:PAD, :] = jnp.zeros((PAD, BLK), jnp.float32)
            st[j, f, PAD + BLK :, :] = jnp.zeros((PAD, BLK), jnp.float32)

    def prepare_and_send(q):
        j = lax.rem(q + 1, block_rows)
        prepare(j)
        loop(sources, lambda i: send(cpk, car, cs, cr, member(row_of(j), i)))

    loop(block_rows, prepare_and_send)
    car[me] = cpk[me]
    car[n] = jnp.zeros(car.shape[1:], jnp.float32)
    bar[n] = jnp.zeros(bar.shape[1:], jnp.float32)

    def inverse(c):
        def look(o, found):
            for s in range(slots):
                found = jnp.where(table[o, s] == base + c, o, found)
            return found

        found = jnp.int32(n)
        if n <= 32:
            for o in range(n):
                found = look(o, found)
        else:
            found = lax.fori_loop(0, n, look, found)
        owner_of[c] = found

    loop(columns, inverse)

    lane = lax.broadcasted_iota(jnp.int32, (STRIP, BLK), 1)
    not_last = lane < BLK - 1
    not_first = lane > 0

    def east(x):
        return jnp.where(not_last, pltpu.roll(x, BLK - 1, 1), 0.0) - jnp.where(
            not_first, pltpu.roll(x, 1, 1), 0.0
        )

    def ice(j):
        row = row_of(j)
        first = row * sources

        def get(f, r, shift=0):
            return st[j, f, pl.ds(PAD + r + shift, STRIP), :]

        def north(f, r):
            return get(f, r, 1) - get(f, r, -1)

        def water(f, r):
            return ar[pl.ds(first + r // rows, STRIP // rows), f].reshape(STRIP, BLK)

        def substep(step):
            for r in range(0, BLK, STRIP):
                cut = pl.ds(r, STRIP)
                eu = east(get(0, r))
                ev = east(get(1, r))
                nu = north(0, r)
                nv = north(1, r)
                div = eu + nv
                ten = eu - nv
                shear = nu + ev
                scale = cf[j, 1, cut, :]
                z = scale * lax.rsqrt(div * div + 0.25 * (ten * ten + shear * shear) + 1.0)
                z4 = 0.25 * z
                mine = pl.ds(PAD + r, STRIP)
                st[j, 2, mine, :] = (1.0 - RELAXATION) * get(2, r) + (z * div - scale)
                st[j, 3, mine, :] = (1.0 - RELAXATION) * get(3, r) + z4 * ten
                st[j, 4, mine, :] = (1.0 - RELAXATION) * get(4, r) + z4 * shear
            for r in range(0, BLK, STRIP):
                cut = pl.ds(r, STRIP)
                fx = 0.25 * east(get(2, r) + get(3, r)) + 0.5 * north(4, r)
                fy = 0.25 * (north(2, r) - north(3, r)) + 0.5 * east(get(4, r))
                u = get(0, r)
                v = get(1, r)
                uo = water(0, r)
                vo = water(1, r)
                total = cf[j, 0, cut, :]
                ru = uo - u
                rv = vo - v
                q = ru * ru + rv * rv + 0.0001
                drag = q * lax.rsqrt(q)
                inertia = total * (1.0 / ICE_STEP)
                turn = CORIOLIS * total
                inv = 1.0 / (inertia + drag)
                mine = pl.ds(PAD + r, STRIP)
                st[j, 0, mine, :] = (inertia * u + fx + drag * uo + turn * v) * inv
                st[j, 1, mine, :] = (inertia * v + fy + drag * vo - turn * u) * inv

        loop(NSUB, substep)
        slot, valid = find(row)
        keep = valid.astype(jnp.float32)
        for r in range(0, BLK, STRIP):
            u = get(0, r)
            v = get(1, r)
            ru = u - water(0, r)
            rv = v - water(1, r)
            q = ru * ru + rv * rv + 0.0001
            drag = keep * (q * lax.rsqrt(q))
            taux = drag * ru
            tauy = drag * rv
            for i in range(STRIP // rows):
                bpk[first + r // rows + i, 0] = taux[i * rows : (i + 1) * rows]
                bpk[first + r // rows + i, 1] = tauy[i * rows : (i + 1) * rows]

    def item(j):
        loop(sources, lambda i: wait_recv(pk, ar, fs, fr, member(row_of(j), i)))
        ice(j)
        loop(sources, lambda i: send(bpk, bar, bs, br, member(row_of(j), i)))

    loop(block_rows, item)
    bar[me] = bpk[me]

    def finish_ice(s):
        block = table[me, s]
        j = jnp.int32(0)
        for other in range(block_rows):
            rel = block - row_of(other) * columns
            j = jnp.where((rel >= 0) & (rel < columns), other, j)
        keep = jnp.where(block >= 0, 1, 0).astype(jnp.float32)
        for f in range(5):
            io[s, f] = keep * st[j, f, pl.ds(PAD, BLK), :]

    loop(slots, finish_ice)
    store_ice = pltpu.make_async_copy(io, ice_o, store_sem.at[0])
    store_ice.start()

    @pl.when(me < n - 1)
    def _():
        halo(0, up).wait_send()
        halo(1, up).wait_recv()

    @pl.when(me > 0)
    def _():
        halo(1, down).wait_send()
        halo(0, down).wait_recv()

    lane_o = lax.broadcasted_iota(jnp.int32, (rows, BLK), 1)
    row_o = lax.broadcasted_iota(jnp.int32, (rows, BLK), 0)

    def tend(c):
        left = lax.rem(c + columns - 1, columns)
        right = lax.rem(c + 1, columns)
        wet = 1.0 - land[base + c].astype(jnp.float32)
        gain = TIME_STEP * wet
        x = [[oc[c, f, k] for k in range(levels)] for f in range(3)]
        for k in range(levels):
            for f in range(3):
                at = f * levels + k
                centre = x[f][k]
                east_cells = jnp.where(
                    lane_o == BLK - 1,
                    pltpu.roll(oc[right, f, k], BLK - 1, 1),
                    pltpu.roll(centre, BLK - 1, 1),
                )
                west_cells = jnp.where(
                    lane_o == 0, pltpu.roll(oc[left, f, k], 1, 1), pltpu.roll(centre, 1, 1)
                )
                upper = jnp.where(
                    row_o == rows - 1, hr[1, c, at : at + 1], pltpu.roll(centre, rows - 1, 0)
                )
                lower = jnp.where(row_o == 0, hr[0, c, at : at + 1], pltpu.roll(centre, 1, 0))
                laplace = upper + lower + east_cells + west_cells - 4.0 * centre
                advection = x[1][k] * (0.5 * (east_cells - west_cells)) + x[2][k] * (
                    0.5 * (upper - lower)
                )
                t = MIX_HORIZ * laplace - advection
                if k + 1 < levels:
                    t = t + MIX_VERT * (x[f][k + 1] - centre)
                if k > 0:
                    t = t + MIX_VERT * (x[f][k - 1] - centre)
                if f == 1:
                    t = t + CORIOLIS * x[2][k]
                if f == 2:
                    t = t - CORIOLIS * x[1][k]
                result = centre + gain * t
                acc[c, f, k] = result * wet if f else result

    loop(columns, tend)

    loop(n, lambda d: wait_recv(cpk, car, cs, cr, d))

    def store_early(c):
        return pltpu.make_async_copy(acc.at[c, 0], ocean_o.at[0, :, :, lanes(c)], early_sem.at[c])

    def store_late(c):
        return pltpu.make_async_copy(
            acc.at[c, 1:3], ocean_o.at[1:3, :, :, lanes(c)], late_sem.at[c]
        )

    def heat(c):
        wet = 1.0 - land[base + c].astype(jnp.float32)
        cover = car[owner_of[c]]
        acc[c, 0, 0] += (TIME_STEP * HEAT_RATE * wet) * (cover * (FREEZING - oc[c, 0, 0]))
        store_early(c).start()

    loop(columns, heat)
    loop(n, lambda d: wait_recv(bpk, bar, bs, br, d))

    def stress(c):
        wet = 1.0 - land[base + c].astype(jnp.float32)
        o = owner_of[c]
        for f in range(2):
            acc[c, 1 + f, 0] += (TIME_STEP * STRESS_GAIN * wet) * bar[o, f]
        store_late(c).start()

    loop(columns, stress)

    def drain(d):
        wait_send(pk, ar, fs, fr, d)
        wait_send(cpk, car, cs, cr, d)
        wait_send(bpk, bar, bs, br, d)

    loop(n, drain)
    store_ice.wait()
    loop(columns, lambda c: store_early(c).wait())
    loop(columns, lambda c: store_late(c).wait())


def shards(n, ocean_state, ice_dynamics, ice_thickness, ice_table, land_mask):
    _, levels, rows, width = ocean_state.shape
    slots = ice_dynamics.shape[0]
    columns = width // BLK
    block_rows = n * rows // BLK
    f32 = jnp.float32
    halo_rows = -(-3 * levels // 8) * 8
    dma = pltpu.SemaphoreType.DMA
    smem = pl.BlockSpec(memory_space=pltpu.SMEM)
    hbm = pl.BlockSpec(memory_space=pl.ANY)
    return pl.pallas_call(
        functools.partial(kernel, n, columns, levels, slots, rows),
        out_shape=(
            jax.ShapeDtypeStruct(ocean_state.shape, f32),
            jax.ShapeDtypeStruct(ice_dynamics.shape, f32),
        ),
        in_specs=[smem, smem, hbm, hbm, hbm],
        out_specs=(hbm, hbm),
        scratch_shapes=[
            pltpu.VMEM((columns, 3, levels, rows, BLK), f32),
            pltpu.VMEM((columns, 3, levels, rows, BLK), f32),
            pltpu.VMEM(ice_dynamics.shape, f32),
            pltpu.VMEM(ice_thickness.shape, f32),
            pltpu.VMEM((2, columns, halo_rows, BLK), f32),
            pltpu.VMEM((2, columns, halo_rows, BLK), f32),
            pltpu.VMEM((n, 2, rows, BLK), f32),
            pltpu.VMEM((n, 2, rows, BLK), f32),
            pltpu.VMEM((n, rows, BLK), f32),
            pltpu.VMEM((n + 1, rows, BLK), f32),
            pltpu.VMEM((n, 2, rows, BLK), f32),
            pltpu.VMEM((n + 1, 2, rows, BLK), f32),
            pltpu.VMEM((block_rows, 5, BLK + 2 * PAD, BLK), f32),
            pltpu.VMEM((block_rows, 2, BLK, BLK), f32),
            pltpu.VMEM(ice_dynamics.shape, f32),
            pltpu.SMEM((columns,), jnp.int32),
            dma((2,)), dma((1,)), dma((columns,)), dma((columns,)), dma((columns,)),
            dma((n,)), dma((n,)), dma((n,)), dma((n,)), dma((n,)), dma((n,)),
            dma((2,)), dma((2,)),
        ],
        compiler_params=pltpu.CompilerParams(
            collective_id=0, has_side_effects=True, vmem_limit_bytes=48 * 1024 * 1024
        ),
    )(ice_table, land_mask, ocean_state, ice_dynamics, ice_thickness)


def solution(mesh):
    in_specs = (
        P(None, "groups", "tiles", None),
        P("tiles", "groups", None, None),
        P("tiles", "groups", None, None),
        P("groups", None),
        P("groups"),
    )
    out_specs = (P(None, "groups", "tiles", None), P("tiles", "groups", None, None))
    return jax.shard_map(
        functools.partial(shards, mesh.shape["tiles"]),
        mesh=mesh, in_specs=in_specs, out_specs=out_specs, check_vma=False,
    )
```

```python
import functools

import jax
import jax.numpy as jnp
from jax import lax
from jax.experimental import pallas as pl
from jax.experimental.pallas import tpu as pltpu
from jax.sharding import PartitionSpec as P

BLK = 128
NSUB = 8
TIME_STEP = 0.1
MIX_HORIZ = 0.5
MIX_VERT = 0.25
CORIOLIS = 0.5
STRESS_GAIN = 2.0
RELAXATION = 0.2
ICE_STEP = 0.5
STRENGTH_SCALE = 0.25
HEAT_RATE = 0.5
FREEZING = -1.0
CATEGORY_WEIGHTS = (0.5, 0.75, 1.0, 1.25, 1.5)
PAD = 8
STRIP = 32
VMEM_BYTES = 64 * 1024 * 1024
MESH = pl.DeviceIdType.MESH


def loop(count, body):
    def step(i, carry):
        body(i)
        return carry

    lax.fori_loop(0, count, step, 0)


def kernel(
    n, columns, levels, slots, rows,
    table_h, land_h, ocean_h, dyn_h, thick_h, acc, io,
    oc, dy, th, hs, hr, pk, ar, cpk, car, bpk, bar, st, cf, owner_of, table, land,
    load_sem, fs, fr, cs, cr, bs, br, hss, hrs,
):
    me = lax.axis_index("tiles")
    sources = BLK // rows
    block_rows = n // sources
    my_row = me // sources
    my_part = lax.rem(me, sources)
    base = my_row * columns

    def lanes(c):
        return pl.ds(pl.multiple_of(c * BLK, BLK), BLK)

    def load_ocean(c):
        return pltpu.make_async_copy(ocean_h.at[:, :, :, lanes(c)], oc.at[c], load_sem.at[2])

    load_table = pltpu.make_async_copy(table_h, table, load_sem.at[3])
    load_land = pltpu.make_async_copy(land_h, land, load_sem.at[4])
    load_table.start()
    load_land.start()
    load_thick = pltpu.make_async_copy(thick_h, th, load_sem.at[0])
    load_dyn = pltpu.make_async_copy(dyn_h, dy, load_sem.at[1])
    loop(columns, lambda c: load_ocean(c).start())
    load_thick.start()
    load_dyn.start()

    barrier = pltpu.get_barrier_semaphore()

    def greet(k):
        peer = lax.rem(me + 1 + k, n)
        pl.semaphore_signal(barrier, inc=1, device_id={"tiles": peer}, device_id_type=MESH)

    loop(n - 1, greet)

    def remote(src, dst, ssem, rsem, slot_there, peer):
        return pltpu.make_async_remote_copy(
            src_ref=src.at[peer], dst_ref=dst.at[slot_there], send_sem=ssem.at[peer],
            recv_sem=rsem.at[slot_there], device_id={"tiles": peer}, device_id_type=MESH,
        )

    def send(src, dst, ssem, rsem, peer):
        @pl.when(peer != me)
        def _():
            remote(src, dst, ssem, rsem, me, peer).start()

    def wait_recv(src, dst, ssem, rsem, peer):
        @pl.when(peer != me)
        def _():
            remote(src, dst, ssem, rsem, peer, peer).wait_recv()

    def wait_send(src, dst, ssem, rsem, peer):
        @pl.when(peer != me)
        def _():
            remote(src, dst, ssem, rsem, me, peer).wait_send()

    def member(row, i):
        return row * sources + lax.rem(my_part + i, sources)

    def row_of(j):
        return lax.rem(my_row + j, block_rows)

    load_table.wait()
    load_land.wait()
    pltpu.make_async_copy(oc, oc, load_sem.at[2]).wait()

    def pack(o):
        col = 0
        for s in range(slots):
            rel = table[s, o] - base
            col = jnp.where((rel >= 0) & (rel < columns), rel, col)
        pk[o, 0] = oc[col, 1, 0]
        pk[o, 1] = oc[col, 2, 0]

    loop(n, pack)
    ar[me] = pk[me]
    blank = jnp.zeros((1, BLK), jnp.float32)

    def edges(c):
        tops = [oc[c, f, k, rows - 1 : rows] for f in range(3) for k in range(levels)]
        ends = [oc[c, f, k, 0:1] for f in range(3) for k in range(levels)]
        more = [blank] * (hs.shape[2] - len(tops))
        hs[0, c] = jnp.concatenate(tops + more, axis=0)
        hs[1, c] = jnp.concatenate(ends + more, axis=0)

    loop(columns, edges)

    pl.semaphore_wait(barrier, n - 1)

    def send_fwd(q):
        send(pk, ar, fs, fr, member(row_of(1 + q // sources), lax.rem(q, sources)))

    loop(n, send_fwd)

    def halo(i, peer):
        return pltpu.make_async_remote_copy(
            src_ref=hs.at[i], dst_ref=hr.at[i], send_sem=hss.at[i], recv_sem=hrs.at[i],
            device_id={"tiles": peer}, device_id_type=MESH,
        )

    up = jnp.minimum(me + 1, n - 1)
    down = jnp.maximum(me - 1, 0)

    @pl.when(me < n - 1)
    def _():
        halo(0, up).start()

    @pl.when(me > 0)
    def _():
        halo(1, down).start()

    @pl.when(me == 0)
    def _():
        hr[0] = jnp.zeros(hr.shape[1:], jnp.float32)

    @pl.when(me == n - 1)
    def _():
        hr[1] = jnp.zeros(hr.shape[1:], jnp.float32)

    def find(row):
        slot = jnp.int32(0)
        valid = jnp.int32(0)
        for s in range(slots):
            rel = table[s, me] - row * columns
            hit = (rel >= 0) & (rel < columns)
            slot = jnp.where(hit, s, slot)
            valid = jnp.where(hit, 1, valid)
        return slot, valid

    load_thick.wait()
    load_dyn.wait()

    def prepare(j):
        row = row_of(j)
        slot, valid = find(row)
        keep = valid.astype(jnp.float32)
        for r in range(0, BLK, STRIP):
            cut = pl.ds(r, STRIP)
            parts = [th[slot, k, cut, :] for k in range(len(CATEGORY_WEIGHTS))]
            total = parts[0]
            weighted = CATEGORY_WEIGHTS[0] * parts[0]
            for weight, part in zip(CATEGORY_WEIGHTS[1:], parts[1:]):
                total = total + part
                weighted = weighted + weight * part
            cf[j, 0, cut, :] = total
            cf[j, 1, cut, :] = (0.5 * RELAXATION * STRENGTH_SCALE) * weighted
            cover = keep * (1.0 - jnp.exp(-total))
            for i in range(STRIP // rows):
                cpk[row * sources + r // rows + i] = cover[i * rows : (i + 1) * rows]
            for f in range(5):
                st[j, f, pl.ds(PAD + r, STRIP), :] = dy[slot, f, cut, :]
        for f in range(5):
            st[j, f, 0:PAD, :] = jnp.zeros((PAD, BLK), jnp.float32)
            st[j, f, PAD + BLK :, :] = jnp.zeros((PAD, BLK), jnp.float32)

    def prepare_and_send(q):
        j = lax.rem(q + 1, block_rows)
        prepare(j)
        loop(sources, lambda i: send(cpk, car, cs, cr, member(row_of(j), i)))

    loop(block_rows, prepare_and_send)
    car[me] = cpk[me]
    car[n] = jnp.zeros(car.shape[1:], jnp.float32)
    bar[n] = jnp.zeros(bar.shape[1:], jnp.float32)

    def inverse(c):
        def look(o, found):
            for s in range(slots):
                found = jnp.where(table[s, o] == base + c, o, found)
            return found

        found = jnp.int32(n)
        if n <= 32:
            for o in range(n):
                found = look(o, found)
        else:
            found = lax.fori_loop(0, n, look, found)
        owner_of[c] = found

    loop(columns, inverse)

    lane = lax.broadcasted_iota(jnp.int32, (STRIP, BLK), 1)
    not_last = lane < BLK - 1
    not_first = lane > 0

    def east(x):
        return jnp.where(not_last, pltpu.roll(x, BLK - 1, 1), 0.0) - jnp.where(
            not_first, pltpu.roll(x, 1, 1), 0.0
        )

    def ice(j):
        row = row_of(j)
        first = row * sources

        def get(f, r, shift=0):
            return st[j, f, pl.ds(PAD + r + shift, STRIP), :]

        def north(f, r):
            return get(f, r, 1) - get(f, r, -1)

        def water(f, r):
            return ar[pl.ds(first + r // rows, STRIP // rows), f].reshape(STRIP, BLK)

        def substep(step):
            for r in range(0, BLK, STRIP):
                cut = pl.ds(r, STRIP)
                eu = east(get(0, r))
                ev = east(get(1, r))
                nu = north(0, r)
                nv = north(1, r)
                div = eu + nv
                ten = eu - nv
                shear = nu + ev
                scale = cf[j, 1, cut, :]
                z = scale * lax.rsqrt(div * div + 0.25 * (ten * ten + shear * shear) + 1.0)
                z4 = 0.25 * z
                mine = pl.ds(PAD + r, STRIP)
                st[j, 2, mine, :] = (1.0 - RELAXATION) * get(2, r) + (z * div - scale)
                st[j, 3, mine, :] = (1.0 - RELAXATION) * get(3, r) + z4 * ten
                st[j, 4, mine, :] = (1.0 - RELAXATION) * get(4, r) + z4 * shear
            for r in range(0, BLK, STRIP):
                cut = pl.ds(r, STRIP)
                fx = 0.25 * east(get(2, r) + get(3, r)) + 0.5 * north(4, r)
                fy = 0.25 * (north(2, r) - north(3, r)) + 0.5 * east(get(4, r))
                u = get(0, r)
                v = get(1, r)
                uo = water(0, r)
                vo = water(1, r)
                total = cf[j, 0, cut, :]
                ru = uo - u
                rv = vo - v
                q = ru * ru + rv * rv + 0.0001
                drag = q * lax.rsqrt(q)
                inertia = total * (1.0 / ICE_STEP)
                turn = CORIOLIS * total
                inv = 1.0 / (inertia + drag)
                mine = pl.ds(PAD + r, STRIP)
                st[j, 0, mine, :] = (inertia * u + fx + drag * uo + turn * v) * inv
                st[j, 1, mine, :] = (inertia * v + fy + drag * vo - turn * u) * inv

        loop(NSUB, substep)
        slot, valid = find(row)
        keep = valid.astype(jnp.float32)
        for r in range(0, BLK, STRIP):
            u = get(0, r)
            v = get(1, r)
            ru = u - water(0, r)
            rv = v - water(1, r)
            q = ru * ru + rv * rv + 0.0001
            drag = keep * (q * lax.rsqrt(q))
            taux = drag * ru
            tauy = drag * rv
            for i in range(STRIP // rows):
                bpk[first + r // rows + i, 0] = taux[i * rows : (i + 1) * rows]
                bpk[first + r // rows + i, 1] = tauy[i * rows : (i + 1) * rows]

    def item(j):
        loop(sources, lambda i: wait_recv(pk, ar, fs, fr, member(row_of(j), i)))
        ice(j)
        loop(sources, lambda i: send(bpk, bar, bs, br, member(row_of(j), i)))

    loop(block_rows, item)
    bar[me] = bpk[me]

    def finish_ice(s):
        block = table[s, me]
        j = jnp.int32(0)
        for other in range(block_rows):
            rel = block - row_of(other) * columns
            j = jnp.where((rel >= 0) & (rel < columns), other, j)
        keep = jnp.where(block >= 0, 1, 0).astype(jnp.float32)
        for f in range(5):
            io[s, f] = keep * st[j, f, pl.ds(PAD, BLK), :]

    loop(slots, finish_ice)
    @pl.when(me < n - 1)
    def _():
        halo(0, up).wait_send()
        halo(1, up).wait_recv()

    @pl.when(me > 0)
    def _():
        halo(1, down).wait_send()
        halo(0, down).wait_recv()

    lane_o = lax.broadcasted_iota(jnp.int32, (rows, BLK), 1)
    row_o = lax.broadcasted_iota(jnp.int32, (rows, BLK), 0)

    def tend(c):
        left = lax.rem(c + columns - 1, columns)
        right = lax.rem(c + 1, columns)
        wet = 1.0 - land[base + c].astype(jnp.float32)
        gain = TIME_STEP * wet
        x = [[oc[c, f, k] for k in range(levels)] for f in range(3)]
        for k in range(levels):
            for f in range(3):
                at = f * levels + k
                centre = x[f][k]
                east_cells = jnp.where(
                    lane_o == BLK - 1,
                    pltpu.roll(oc[right, f, k], BLK - 1, 1),
                    pltpu.roll(centre, BLK - 1, 1),
                )
                west_cells = jnp.where(
                    lane_o == 0, pltpu.roll(oc[left, f, k], 1, 1), pltpu.roll(centre, 1, 1)
                )
                upper = jnp.where(
                    row_o == rows - 1, hr[1, c, at : at + 1], pltpu.roll(centre, rows - 1, 0)
                )
                lower = jnp.where(row_o == 0, hr[0, c, at : at + 1], pltpu.roll(centre, 1, 0))
                laplace = upper + lower + east_cells + west_cells - 4.0 * centre
                advection = x[1][k] * (0.5 * (east_cells - west_cells)) + x[2][k] * (
                    0.5 * (upper - lower)
                )
                t = MIX_HORIZ * laplace - advection
                if k + 1 < levels:
                    t = t + MIX_VERT * (x[f][k + 1] - centre)
                if k > 0:
                    t = t + MIX_VERT * (x[f][k - 1] - centre)
                if f == 1:
                    t = t + CORIOLIS * x[2][k]
                if f == 2:
                    t = t - CORIOLIS * x[1][k]
                result = centre + gain * t
                acc[c, f, k] = result * wet if f else result

    loop(columns, tend)

    loop(n, lambda d: wait_recv(cpk, car, cs, cr, d))

    def heat(c):
        wet = 1.0 - land[base + c].astype(jnp.float32)
        cover = car[owner_of[c]]
        acc[c, 0, 0] += (TIME_STEP * HEAT_RATE * wet) * (cover * (FREEZING - oc[c, 0, 0]))

    loop(columns, heat)
    loop(n, lambda d: wait_recv(bpk, bar, bs, br, d))

    def stress(c):
        wet = 1.0 - land[base + c].astype(jnp.float32)
        o = owner_of[c]
        for f in range(2):
            acc[c, 1 + f, 0] += (TIME_STEP * STRESS_GAIN * wet) * bar[o, f]

    loop(columns, stress)

    def drain(d):
        wait_send(pk, ar, fs, fr, d)
        wait_send(cpk, car, cs, cr, d)
        wait_send(bpk, bar, bs, br, d)

    loop(n, drain)


def settle(acc, io, ocean_o, ice_o, sems):
    columns = acc.shape[0]
    slots = io.shape[0]
    store_ice = [
        pltpu.make_async_copy(io.at[s], ice_o.at[s], sems.at[1 + s]) for s in range(slots)
    ]
    for copy in store_ice:
        copy.start()

    def store(c):
        lanes = pl.ds(pl.multiple_of(c * BLK, BLK), BLK)
        pltpu.make_async_copy(acc.at[c], ocean_o.at[:, :, :, lanes], sems.at[0]).start()

    loop(columns, store)
    pltpu.make_async_copy(acc, acc, sems.at[0]).wait()
    for copy in store_ice:
        copy.wait()


def shards(n, ocean_state, ice_dynamics, ice_thickness, ice_table, land_mask):
    _, levels, rows, width = ocean_state.shape
    slots = ice_dynamics.shape[0]
    columns = width // BLK
    block_rows = n * rows // BLK
    f32 = jnp.float32
    kept = 4 * (ocean_state.size + ice_dynamics.size) + 384 * 1024
    halo_rows = -(-3 * levels // 8) * 8
    dma = pltpu.SemaphoreType.DMA
    vmem = pl.BlockSpec(memory_space=pltpu.VMEM)
    hbm = pl.BlockSpec(memory_space=pltpu.HBM)
    anywhere = pl.BlockSpec(memory_space=pl.ANY)
    ocean_next, ice_next = pl.pallas_call(
        functools.partial(kernel, n, columns, levels, slots, rows),
        out_shape=(
            pltpu.VMEM((columns, 3, levels, rows, BLK), f32),
            pltpu.VMEM(ice_dynamics.shape, f32),
        ),
        in_specs=[hbm, hbm, hbm, hbm, hbm],
        out_specs=(vmem, vmem),
        scratch_shapes=[
            pltpu.VMEM((columns, 3, levels, rows, BLK), f32),
            pltpu.VMEM(ice_dynamics.shape, f32),
            pltpu.VMEM(ice_thickness.shape, f32),
            pltpu.VMEM((2, columns, halo_rows, BLK), f32),
            pltpu.VMEM((2, columns, halo_rows, BLK), f32),
            pltpu.VMEM((n, 2, rows, BLK), f32),
            pltpu.VMEM((n, 2, rows, BLK), f32),
            pltpu.VMEM((n, rows, BLK), f32),
            pltpu.VMEM((n + 1, rows, BLK), f32),
            pltpu.VMEM((n, 2, rows, BLK), f32),
            pltpu.VMEM((n + 1, 2, rows, BLK), f32),
            pltpu.VMEM((block_rows, 5, BLK + 2 * PAD, BLK), f32),
            pltpu.VMEM((block_rows, 2, BLK, BLK), f32),
            pltpu.SMEM((columns,), jnp.int32),
            pltpu.SMEM((slots, n), jnp.int32),
            pltpu.SMEM(land_mask.shape, jnp.int32),
            dma((5,)),
            dma((n,)), dma((n,)), dma((n,)), dma((n,)), dma((n,)), dma((n,)),
            dma((2,)), dma((2,)),
        ],
        compiler_params=pltpu.CompilerParams(
            collective_id=0, has_side_effects=True, vmem_limit_bytes=VMEM_BYTES - kept
        ),
    )(ice_table.T, land_mask, ocean_state, ice_dynamics, ice_thickness)
    return pl.pallas_call(
        settle,
        out_shape=(
            jax.ShapeDtypeStruct(ocean_state.shape, f32),
            jax.ShapeDtypeStruct(ice_dynamics.shape, f32),
        ),
        in_specs=[anywhere, anywhere],
        out_specs=(hbm, hbm),
        scratch_shapes=[dma((1 + slots,))],
        compiler_params=pltpu.CompilerParams(vmem_limit_bytes=1024 * 1024),
    )(ocean_next, ice_next)


def solution(mesh):
    in_specs = (
        P(None, "groups", "tiles", None),
        P("tiles", "groups", None, None),
        P("tiles", "groups", None, None),
        P("groups", None),
        P("groups"),
    )
    out_specs = (P(None, "groups", "tiles", None), P("tiles", "groups", None, None))
    return jax.shard_map(
        functools.partial(shards, mesh.shape["tiles"]),
        mesh=mesh, in_specs=in_specs, out_specs=out_specs, check_vma=False,
    )
```
